32 devices in a mesh: grp: 2 (over x), dev: 16 (over z, y, core).
Axes of the slice: x: 2, y: 2, z: 4, core: 2. Of those that a mesh axis runs over, the one named last changes fastest.
Arguments:
- step_number: int32 [], replicated, may hold values from 0 to 999
- power_maps: bfloat16 [256, 64, 128], P(('grp', 'dev')), may hold values from -6 to 6
- heat_maps: bfloat16 [256, 1024], P(('grp', 'dev')), may hold values from -6 to 6
- home_table: int32 [2, 128], P('grp'), may hold values from 0 to 127, as said below
- requests: int32 [32, 32], P(('grp', 'dev')), may hold values from 0 to 127, as said below
- counts: int32 [32], P(('grp', 'dev')), may hold values from 1 to 32, as said below
- stem_weight: float32 [32, 128, 256], P(('grp', 'dev')), may hold values from -0.5 to 0.5
- conv_weight: float32 [32, 2, 2304, 256], P(('grp', 'dev')), may hold values from -0.125 to 0.125
- head_weight: float32 [32, 16, 256], P(('grp', 'dev')), may hold values from -0.375 to 0.375
- biases: float32 [32, 3, 256], P(('grp', 'dev')), may hold values from -3 to 3
Outputs:
- new_stem: float32 [32, 128, 256], P(('grp', 'dev'))
- new_conv: float32 [32, 2, 2304, 256], P(('grp', 'dev'))
- new_head: float32 [32, 16, 256], P(('grp', 'dev'))
- new_biases: float32 [32, 3, 256], P(('grp', 'dev'))
- grad_stem: bfloat16 [32, 128, 256], P(('grp', 'dev'))
- grad_conv: bfloat16 [32, 2, 2304, 256], P(('grp', 'dev'))
- grad_head: bfloat16 [32, 16, 256], P(('grp', 'dev'))
- grad_biases: bfloat16 [32, 3, 256], P(('grp', 'dev'))
The draws below stay inside these ranges and needn't reach their ends.
Inputs may be any that keep to these rules, and one draw needn't show every extreme that they name: Each row is a permutation; sample s of group g is stored by dev index home_table[g, s] // 8 as its local sample home_table[g, s] % 8. Among the live requests of one device (its first counts entries) at most 2 are stored by any one dev index; in every group some device has exactly 2 from one dev index. `counts`: in every group some device has 32 live requests.
All inputs are finite; a program needn't handle non-finite values.
Results may differ from the reference program's by a relative error of at most 0.024.
The reference program's roundings to bfloat16 on the way (of `stem_act`, `inner_act` and `block_out`) count: a program that leaves them out, or rounds other values in their place, can miss the bound.
Values may be sent and summed in bfloat16 or wider, within the bound.
A program may use at most 128 MiB of HBM per device.

```python
import jax
import jax.numpy as jnp
from jax import lax

C = 256
FEAT = 128
OUTPIX = 16
PH = 8
PW = 8
S_DEV = 8
REQ = 32
GROUPS = 2
PEERS = 16
GSAMPLES = 128
DEVICES = 32


def make_tables(key):
    folded = jax.random.fold_in(key, 11)
    key_home, key_owner, key_local, key_second, key_first, key_other, key_order, key_full = jax.random.split(folded, 8)
    home_table = jax.vmap(lambda single: jax.random.permutation(single, GSAMPLES))(jax.random.split(key_home, GROUPS)).astype(jnp.int32)
    inverse = jnp.argsort(home_table, axis=1).astype(jnp.int32)
    half_req = REQ // 2
    owner_perm = jax.vmap(lambda single: jax.random.permutation(single, PEERS))(jax.random.split(key_owner, DEVICES))[:, :half_req]
    owner_list = jnp.concatenate([owner_perm, owner_perm], axis=1).astype(jnp.int32)
    local_base = jax.random.randint(key_local, (DEVICES, half_req), 0, S_DEV)
    second = (local_base + 1 + jax.random.randint(key_second, (DEVICES, half_req), 0, S_DEV - 1)) % S_DEV
    local_list = jnp.concatenate([local_base, second], axis=1).astype(jnp.int32)
    shuffle = jax.vmap(lambda single: jax.random.permutation(single, REQ))(jax.random.split(key_order, DEVICES))
    owner_list = jnp.take_along_axis(owner_list, shuffle, axis=1)
    local_list = jnp.take_along_axis(local_list, shuffle, axis=1)
    position = owner_list * S_DEV + local_list
    group_of = jnp.arange(DEVICES, dtype=jnp.int32) // PEERS
    requests = jnp.take_along_axis(inverse[group_of], position, axis=1).astype(jnp.int32)
    first_draw = jax.random.randint(key_first, (DEVICES,), half_req, REQ + 1)
    other_draw = jax.random.randint(key_other, (DEVICES,), half_req, REQ + 1)
    chosen = jax.random.randint(key_full, (GROUPS,), 0, PEERS)
    counts = jnp.where(jnp.arange(DEVICES, dtype=jnp.int32) % PEERS == chosen[group_of], REQ, jnp.maximum(first_draw, other_draw))
    return (home_table, requests, counts.astype(jnp.int32))


def draw_home_table(key, part):
    return make_tables(key)[0]


def draw_requests(key, part):
    return make_tables(key)[1]


def draw_counts(key, part):
    return make_tables(key)[2]


def steps_of(rng, shape, cuts, least, largest):
    def one(axis_at, parts):
        heights = jax.random.uniform(jax.random.fold_in(jax.random.fold_in(rng, 6), axis_at), (parts,), jnp.float32, least / len(cuts), largest / len(cuts))
        return jnp.repeat(jnp.exp(heights), shape[axis_at] // parts).reshape((-1,) + (1,) * (len(shape) - axis_at - 1))

    gain = one(*cuts[0])
    for cut in cuts[1:]:
        gain = gain * one(*cut)
    return gain


def scatter_about(key, extent, scale, most, pieces=(), kind=jnp.bfloat16):
    result = jax.random.normal(key, extent, jnp.float32) * scale
    if len(pieces) > 0:
        result = steps_of(key, extent, pieces, -0.22, 0.18) * result
    return jnp.clip(result, min=-most, max=most).astype(kind)


def setup_inputs(seed: int = 0) -> dict:
    arg_keys = jax.random.split(jax.random.key(seed), 11)
    step_number = jax.random.randint(arg_keys[0], (), 0, 1000).astype(jnp.int32)
    power_maps = scatter_about(arg_keys[1], (DEVICES * S_DEV, PH * PW, FEAT), 1.0, 6.0, ((0, 32),))
    heat_maps = scatter_about(arg_keys[2], (DEVICES * S_DEV, PH * PW * OUTPIX), 1.0, 6.0, ((0, 32),))
    home_table = draw_home_table(jax.random.fold_in(arg_keys[10], 71), 0)
    requests = draw_requests(jax.random.fold_in(arg_keys[10], 71), 0)
    counts = draw_counts(jax.random.fold_in(arg_keys[10], 71), 0)
    stem_weight = scatter_about(arg_keys[6], (DEVICES, FEAT, C), FEAT ** -0.5, 0.5, ((0, 32),), jnp.float32)
    conv_weight = scatter_about(arg_keys[7], (DEVICES, 2, 9 * C, C), (9 * C) ** -0.5, 0.125, ((0, 32),), jnp.float32)
    head_weight = scatter_about(arg_keys[8], (DEVICES, OUTPIX, C), C ** -0.5, 0.375, ((0, 32),), jnp.float32)
    biases = scatter_about(arg_keys[9], (DEVICES, 3, C), 0.5, 3.0, ((0, 32),), jnp.float32)
    return {"step_number": step_number, "power_maps": power_maps, "heat_maps": heat_maps, "home_table": home_table, "requests": requests, "counts": counts, "stem_weight": stem_weight, "conv_weight": conv_weight, "head_weight": head_weight, "biases": biases}


LEARN_RATE = 0.1

def conv_three(activation, weight, height, width):
    batch_size, positions, channels = activation.shape
    grid_map = activation.reshape(batch_size, height, width, channels)
    padded = jnp.pad(grid_map, ((0, 0), (1, 1), (1, 1), (0, 0)))
    columns = jnp.concatenate([padded[:, row_shift:row_shift + height, col_shift:col_shift + width, :] for row_shift in range(3) for col_shift in range(3)], axis=3)
    product = jnp.dot(columns.reshape(batch_size * positions, 9 * channels), weight, preferred_element_type=jnp.float32)
    return product.reshape(batch_size, positions, channels)

def batch_loss(params, power_maps, heat_maps, alive_mask, sample_count, height, width):
    stem_weight, conv_weight, head_weight, biases = params
    batch_size, positions, features = power_maps.shape
    channels = stem_weight.shape[1]
    stem_pre = jnp.dot(power_maps.reshape(batch_size * positions, features), stem_weight.astype(jnp.bfloat16), preferred_element_type=jnp.float32) + biases[0]
    stem_act = jax.nn.relu(stem_pre).astype(jnp.bfloat16).reshape(batch_size, positions, channels)
    inner_act = jax.nn.relu(conv_three(stem_act, conv_weight[0].astype(jnp.bfloat16), height, width) + biases[1]).astype(jnp.bfloat16)
    branch_out = conv_three(inner_act, conv_weight[1].astype(jnp.bfloat16), height, width) + biases[2]
    block_out = jax.nn.relu(stem_act.astype(jnp.float32) + branch_out).astype(jnp.bfloat16)
    predicted = lax.dot_general(block_out.reshape(batch_size * positions, channels), head_weight.astype(jnp.bfloat16), (((1,), (1,)), ((), ())), preferred_element_type=jnp.float32).reshape(batch_size, -1)
    error_map = (predicted - heat_maps.astype(jnp.float32)) * alive_mask[:, None]
    return jnp.sum(error_map * error_map) / (sample_count * error_map.shape[1])

def reference(step_number, power_maps, heat_maps, home_table, requests, counts, stem_weight, conv_weight, head_weight, biases):
    bit_count = DEVICES.bit_length() - 1
    flip_mask = jnp.left_shift(jnp.int32(1), (step_number % bit_count).astype(jnp.int32))

    def per_device(device):
        group_of = device // PEERS
        position = jnp.take(home_table[group_of], requests[device], axis=0)
        source_rows = (group_of * GSAMPLES + position).astype(jnp.int32)
        batch_maps = jnp.take(power_maps, source_rows, axis=0)
        batch_heat = jnp.take(heat_maps, source_rows, axis=0)
        alive_mask = (jnp.arange(REQ, dtype=jnp.int32) < counts[device]).astype(jnp.float32)
        params = (stem_weight[device], conv_weight[device], head_weight[device], biases[device])
        gradients = jax.grad(batch_loss)(params, batch_maps, batch_heat, alive_mask, counts[device].astype(jnp.float32), PH, PW)
        partner = jnp.bitwise_xor(device, flip_mask)
        theirs_all = (stem_weight[partner], conv_weight[partner], head_weight[partner], biases[partner])
        updated = tuple((0.5 * (mine + theirs) - LEARN_RATE * gradient for mine, theirs, gradient in zip(params, theirs_all, gradients)))
        return updated + tuple((gradient.astype(jnp.bfloat16) for gradient in gradients))
    results = lax.map(per_device, jnp.arange(DEVICES, dtype=jnp.int32))
    return (results[0], results[1], results[2], results[3], results[4], results[5], results[6], results[7])
```

```python
import functools

import jax
import jax.numpy as jnp
from jax import lax
from jax.experimental import pallas as pl
from jax.experimental.pallas import tpu as pltpu
from jax.sharding import PartitionSpec as P

PH = 8
PW = 8
CAP = 2
LANES = 128


LEARN_RATE = 0.1


def as_sent(array):
    return jax.tree.map(lambda a: a.astype(jnp.bfloat16) if a.dtype == jnp.float32 else a, array)


def partner_2(array, axis, distance):
    return lax.ppermute(array, axis, [(i, i ^ 1 << distance) for i in range(lax.axis_size(axis))])


def dot_f32(a, b):
    return jnp.dot(a, b, preferred_element_type=jnp.float32)


def step_kernel(
    x_ref,
    heat_ref,
    scale_ref,
    stem_ref,
    conv_ref,
    head_ref,
    bias_ref,
    g_stem,
    g_conv,
    g_head,
    g_bias,
    stem_pad,
    inner_pad,
    dy2_pad,
    dy1_pad,
    turned,
    dy_turned,
    head_sum,
    stem_sum,
    *,
    height,
    width,
    step,
):
    requests, channels = stem_pad.shape[2:]
    rows = step * width * requests
    for pad in (stem_pad, inner_pad, dy2_pad, dy1_pad):
        edge_row = jnp.zeros((1,) + pad.shape[1:], pad.dtype)
        edge_col = jnp.zeros((pad.shape[0], 1) + pad.shape[2:], pad.dtype)
        pad[0:1] = edge_row
        pad[height + 1 : height + 2] = edge_row
        pad[:, 0:1] = edge_col
        pad[:, width + 1 : width + 2] = edge_col
    g_bias[...] = jnp.zeros_like(g_bias)
    head_sum[...] = jnp.zeros_like(head_sum)
    stem_sum[...] = jnp.zeros_like(stem_sum)

    def inside(pad, at):
        return pad.at[pl.ds(at + 1, step), 1 : width + 1]

    def put(pad, at, value):
        inside(pad, at)[...] = value.reshape(step, width, requests, channels)

    def get(pad, at):
        return inside(pad, at)[...].reshape(rows, channels)

    def windows(pad, at):
        return jnp.concatenate(
            [
                pad[pl.ds(at + i, step), j : j + width].reshape(rows, channels)
                for i in range(3)
                for j in range(3)
            ],
            axis=1,
        )

    def turn(which):
        for tap in range(9):
            turned[tap * channels : (tap + 1) * channels, :] = conv_ref[
                which, (8 - tap) * channels : (9 - tap) * channels, :
            ].T

    def over_rows(body):
        def one(chunk, carry):
            body(chunk * step, pl.multiple_of(chunk * rows, rows))
            return carry

        lax.fori_loop(0, height // step, one, 0)

    def weight_gradient(pad, which):
        def one(i, carry):
            for j in range(3):
                window = pad[pl.ds(i, height), j : j + width].reshape(-1, channels)
                product = dot_f32(dy_turned[...], window)
                start = pl.multiple_of((i * 3 + j) * channels, channels)
                g_conv[which, pl.ds(start, channels), :] = product.T.astype(g_conv.dtype)
            return carry

        lax.fori_loop(0, 3, one, 0)

    def hold(which, dy, pad, at, row):
        g_bias[which : which + 1, :] += jnp.sum(dy.astype(jnp.float32), axis=0, keepdims=True)
        if pad is not None:
            put(pad, at, dy)
            dy_turned[:, pl.ds(row, rows)] = dy.T

    def stem_rows(at, row):
        x = x_ref[pl.ds(row, rows), :]
        put(stem_pad, at, jax.nn.relu(dot_f32(x, stem_ref[...]) + bias_ref[0:1, :]).astype(x.dtype))

    def inner_rows(at, row):
        pre = dot_f32(windows(stem_pad, at), conv_ref[0]) + bias_ref[1:2, :]
        put(inner_pad, at, jax.nn.relu(pre).astype(inner_pad.dtype))

    def out_rows(at, row):
        branch = dot_f32(windows(inner_pad, at), conv_ref[1]) + bias_ref[2:3, :]
        block = jax.nn.relu(get(stem_pad, at).astype(jnp.float32) + branch).astype(jnp.bfloat16)
        predicted = lax.dot_general(
            block, head_ref[...], (((1,), (1,)), ((), ())), preferred_element_type=jnp.float32
        )
        error = predicted - heat_ref[pl.ds(row, rows), :].astype(jnp.float32)
        d_predicted = (error.reshape(step * width, requests, -1) * scale_ref[...][None]).reshape(
            rows, -1
        )
        d_predicted = d_predicted.astype(jnp.bfloat16)
        head_sum[...] += dot_f32(d_predicted.T, block)
        d_block = dot_f32(d_predicted, head_ref[...])
        dy = jnp.where(block.astype(jnp.float32) > 0, d_block, 0.0).astype(jnp.bfloat16)
        hold(2, dy, dy2_pad, at, row)

    def d_inner_rows(at, row):
        d_inner = dot_f32(windows(dy2_pad, at), turned[...])
        live = get(inner_pad, at).astype(jnp.float32) > 0
        hold(1, jnp.where(live, d_inner, 0.0).astype(jnp.bfloat16), dy1_pad, at, row)

    def d_stem_rows(at, row):
        d_stem = dot_f32(windows(dy1_pad, at), turned[...]) + get(dy2_pad, at).astype(jnp.float32)
        live = get(stem_pad, at).astype(jnp.float32) > 0
        dy = jnp.where(live, d_stem, 0.0).astype(jnp.bfloat16)
        hold(0, dy, None, at, row)
        stem_sum[...] += dot_f32(x_ref[pl.ds(row, rows), :].T, dy)

    over_rows(stem_rows)
    over_rows(inner_rows)
    over_rows(out_rows)
    g_head[...] = head_sum[...].astype(g_head.dtype)
    weight_gradient(inner_pad, 1)
    turn(1)
    over_rows(d_inner_rows)
    weight_gradient(stem_pad, 0)
    turn(0)
    over_rows(d_stem_rows)
    g_stem[...] = stem_sum[...].astype(g_stem.dtype)


def gradients_of(params, maps, heat, alive, count, height, width):
    stem_weight, conv_weight, head_weight, biases = params
    positions, requests, features = maps.shape
    pixels, channels = head_weight.shape
    lanes = -(-pixels // LANES) * LANES
    total = positions * requests
    scale = alive * (2.0 / (count * (positions * pixels)))
    scale = jnp.pad(jnp.broadcast_to(scale[:, None], (requests, pixels)), ((0, 0), (0, lanes - pixels)))
    heat = jnp.pad(heat.reshape(total, pixels), ((0, 0), (0, lanes - pixels)))
    head = jnp.pad(head_weight, ((0, lanes - pixels), (0, 0)))
    padded = pltpu.VMEM((height + 2, width + 2, requests, channels), jnp.bfloat16)
    flops = 2 * total * channels * (6 * 9 * channels + 2 * features + 3 * lanes)
    g_stem, g_conv, g_head, g_bias = pl.pallas_call(
        functools.partial(step_kernel, height=height, width=width, step=2),
        out_shape=(
            jax.ShapeDtypeStruct(stem_weight.shape, jnp.bfloat16),
            jax.ShapeDtypeStruct(conv_weight.shape, jnp.bfloat16),
            jax.ShapeDtypeStruct(head.shape, jnp.bfloat16),
            jax.ShapeDtypeStruct(biases.shape, jnp.float32),
        ),
        in_specs=[pl.BlockSpec(memory_space=pltpu.VMEM)] * 7,
        out_specs=(pl.BlockSpec(memory_space=pltpu.VMEM),) * 4,
        scratch_shapes=[
            padded,
            padded,
            padded,
            padded,
            pltpu.VMEM((9 * channels, channels), jnp.bfloat16),
            pltpu.VMEM((channels, total), jnp.bfloat16),
            pltpu.VMEM(head.shape, jnp.float32),
            pltpu.VMEM(stem_weight.shape, jnp.float32),
        ],
        compiler_params=pltpu.CompilerParams(vmem_limit_bytes=48 * 2**20),
        cost_estimate=pl.CostEstimate(flops=flops, bytes_accessed=8 * 2**20, transcendentals=0),
    )(maps.reshape(total, features), heat, scale, stem_weight, conv_weight, head, biases)
    return g_stem, g_conv, g_head[:pixels], g_bias


def route_requests(request_row, sample_count, home_row, store_size, slot_cap):
    lookup = request_row[:, None] == jnp.arange(home_row.shape[0], dtype=jnp.int32)[None, :]
    position = jnp.sum(jnp.where(lookup, home_row[None, :], 0), axis=1)
    owner_of = position // store_size
    local_of = position % store_size
    order_ids = jnp.arange(request_row.shape[0], dtype=jnp.int32)
    alive = order_ids < sample_count
    earlier = (
        (owner_of[:, None] == owner_of[None, :])
        & alive[None, :]
        & (order_ids[None, :] < order_ids[:, None])
    )
    slot_of = jnp.minimum(jnp.sum(earlier.astype(jnp.int32), axis=1), slot_cap - 1)
    return (owner_of, local_of, alive, slot_of)


def local(
    step_number,
    power_maps,
    heat_maps,
    home_table,
    requests,
    counts,
    stem_weight,
    conv_weight,
    head_weight,
    biases,
):
    n_dev = lax.axis_size("dev")
    store_size = power_maps.shape[0]
    home_row = home_table[0]
    owner_of, local_of, alive, slot_of = route_requests(
        requests[0], counts[0], home_row, store_size, CAP
    )
    slot_ids = jnp.arange(CAP, dtype=jnp.int32)
    owner_ids = jnp.arange(n_dev, dtype=jnp.int32)
    wanted = (
        (owner_of[:, None, None] == owner_ids[None, :, None])
        & alive[:, None, None]
        & (slot_of[:, None, None] == slot_ids[None, None, :])
    )
    asked = jnp.sum(jnp.where(wanted, local_of[:, None, None] + 1, 0), axis=0) - 1
    shard_params = (stem_weight, conv_weight, head_weight, biases)
    sent_params = as_sent(shard_params)
    bit_total = (n_dev * lax.axis_size("grp")).bit_length() - 1
    selector = step_number % bit_total

    def branch(bit_number, sent):
        partner = partner_2(sent, ("grp", "dev"), bit_number)
        send_table = lax.all_to_all(asked, "dev", split_axis=0, concat_axis=0, tiled=True).reshape(-1)
        stored = jnp.arange(store_size, dtype=jnp.int32)
        chosen = (send_table[:, None] == stored[None, :]).astype(power_maps.dtype)
        shelf = jnp.concatenate([power_maps.reshape(store_size, -1), heat_maps], axis=1)
        parcel = jnp.dot(chosen, shelf, preferred_element_type=jnp.float32).astype(shelf.dtype)
        got = lax.all_to_all(parcel, "dev", split_axis=0, concat_axis=0, tiled=True)
        slots = jnp.arange(got.shape[0], dtype=jnp.int32)
        pick = (((owner_of * CAP + slot_of)[:, None] == slots[None, :]) & alive[:, None]).astype(
            got.dtype
        )
        batch = jnp.dot(pick, got, preferred_element_type=jnp.float32).astype(got.dtype)
        positions, features = power_maps.shape[1:]
        split = positions * features
        maps = batch[:, :split].reshape(-1, positions, features).swapaxes(0, 1)
        heat = batch[:, split:].reshape(batch.shape[0], positions, -1).swapaxes(0, 1)
        gradients = gradients_of(
            (sent[0][0], sent[1][0], sent[2][0], biases[0]),
            maps,
            heat,
            alive.astype(jnp.float32),
            counts[0].astype(jnp.float32),
            PH,
            PW,
        )
        updated = tuple(
            0.5 * (mine + theirs.astype(jnp.float32)) - LEARN_RATE * gradient[None].astype(jnp.float32)
            for mine, theirs, gradient in zip(shard_params, partner, gradients)
        )
        return updated + tuple(gradient[None].astype(jnp.bfloat16) for gradient in gradients)

    return lax.switch(
        selector, [functools.partial(branch, bit) for bit in range(bit_total)], sent_params
    )


def solution(mesh):
    placed = (
        P(),
        P(("grp", "dev"), None, None),
        P(("grp", "dev"), None),
        P("grp", None),
        P(("grp", "dev"), None),
        P(("grp", "dev")),
        P(("grp", "dev"), None, None),
        P(("grp", "dev"), None, None, None),
        P(("grp", "dev"), None, None),
        P(("grp", "dev"), None, None),
    )
    return jax.shard_map(
        local,
        mesh=mesh,
        in_specs=placed,
        out_specs=(
            P(("grp", "dev"), None, None),
            P(("grp", "dev"), None, None, None),
            P(("grp", "dev"), None, None),
            P(("grp", "dev"), None, None),
            P(("grp", "dev"), None, None),
            P(("grp", "dev"), None, None, None),
            P(("grp", "dev"), None, None),
            P(("grp", "dev"), None, None),
        ),
        check_vma=False,
    )
```

```python
import functools

import jax
import jax.numpy as jnp
from jax import lax
from jax.experimental import pallas as pl
from jax.experimental.pallas import tpu as pltpu
from jax.sharding import PartitionSpec as P

PH = 8
PW = 8
CAP = 2
LANES = 128


LEARN_RATE = 0.1


def as_sent(array):
    return jax.tree.map(lambda a: a.astype(jnp.bfloat16) if a.dtype == jnp.float32 else a, array)


def partner_2(array, axis, distance):
    return lax.ppermute(array, axis, [(i, i ^ 1 << distance) for i in range(lax.axis_size(axis))])


def dot_f32(a, b):
    return jnp.dot(a, b, preferred_element_type=jnp.float32)


def step_kernel(
    x_ref,
    heat_ref,
    scale_ref,
    stem_ref,
    conv_ref,
    head_ref,
    bias_ref,
    g_stem,
    g_conv,
    g_head,
    g_bias,
    stem_pad,
    inner_pad,
    dy2_pad,
    dy1_pad,
    turned,
    dy_turned,
    head_sum,
    stem_sum,
    *,
    height,
    width,
    step,
):
    requests, channels = stem_pad.shape[2:]
    rows = step * width * requests
    for pad in (stem_pad, inner_pad, dy2_pad, dy1_pad):
        edge_row = jnp.zeros((1,) + pad.shape[1:], pad.dtype)
        edge_col = jnp.zeros((pad.shape[0], 1) + pad.shape[2:], pad.dtype)
        pad[0:1] = edge_row
        pad[height + 1 : height + 2] = edge_row
        pad[:, 0:1] = edge_col
        pad[:, width + 1 : width + 2] = edge_col
    g_bias[...] = jnp.zeros_like(g_bias)
    head_sum[...] = jnp.zeros_like(head_sum)
    stem_sum[...] = jnp.zeros_like(stem_sum)

    def inside(pad, at):
        return pad.at[pl.ds(at + 1, step), 1 : width + 1]

    def put(pad, at, value):
        inside(pad, at)[...] = value.reshape(step, width, requests, channels)

    def get(pad, at):
        return inside(pad, at)[...].reshape(rows, channels)

    def windows(pad, at):
        return jnp.concatenate(
            [
                pad[pl.ds(at + i, step), j : j + width].reshape(rows, channels)
                for i in range(3)
                for j in range(3)
            ],
            axis=1,
        )

    def turn(which):
        for tap in range(9):
            turned[tap * channels : (tap + 1) * channels, :] = conv_ref[
                which, (8 - tap) * channels : (9 - tap) * channels, :
            ].T

    def over_rows(body):
        def one(chunk, carry):
            body(chunk * step, pl.multiple_of(chunk * rows, rows))
            return carry

        lax.fori_loop(0, height // step, one, 0)

    def weight_gradient(pad, which):
        def one(i, carry):
            for j in range(3):
                window = pad[pl.ds(i, height), j : j + width].reshape(-1, channels)
                product = dot_f32(dy_turned[...], window)
                start = pl.multiple_of((i * 3 + j) * channels, channels)
                g_conv[which, pl.ds(start, channels), :] = product.T.astype(g_conv.dtype)
            return carry

        lax.fori_loop(0, 3, one, 0)

    def hold(which, dy, pad, at, row):
        g_bias[which : which + 1, :] += jnp.sum(dy.astype(jnp.float32), axis=0, keepdims=True)
        if pad is not None:
            put(pad, at, dy)
            dy_turned[:, pl.ds(row, rows)] = dy.T

    def stem_rows(at, row):
        x = x_ref[pl.ds(row, rows), :]
        put(stem_pad, at, jax.nn.relu(dot_f32(x, stem_ref[...]) + bias_ref[0:1, :]).astype(x.dtype))

    def inner_rows(at, row):
        pre = dot_f32(windows(stem_pad, at), conv_ref[0]) + bias_ref[1:2, :]
        put(inner_pad, at, jax.nn.relu(pre).astype(inner_pad.dtype))

    def out_rows(at, row):
        branch = dot_f32(windows(inner_pad, at), conv_ref[1]) + bias_ref[2:3, :]
        block = jax.nn.relu(get(stem_pad, at).astype(jnp.float32) + branch).astype(jnp.bfloat16)
        predicted = lax.dot_general(
            block, head_ref[...], (((1,), (1,)), ((), ())), preferred_element_type=jnp.float32
        )
        error = predicted - heat_ref[pl.ds(row, rows), :].astype(jnp.float32)
        d_predicted = (error.reshape(step * width, requests, -1) * scale_ref[...][None]).reshape(
            rows, -1
        )
        d_predicted = d_predicted.astype(jnp.bfloat16)
        head_sum[...] += dot_f32(d_predicted.T, block)
        d_block = dot_f32(d_predicted, head_ref[...])
        dy = jnp.where(block.astype(jnp.float32) > 0, d_block, 0.0).astype(jnp.bfloat16)
        hold(2, dy, dy2_pad, at, row)

    def d_inner_rows(at, row):
        d_inner = dot_f32(windows(dy2_pad, at), turned[...])
        live = get(inner_pad, at).astype(jnp.float32) > 0
        hold(1, jnp.where(live, d_inner, 0.0).astype(jnp.bfloat16), dy1_pad, at, row)

    def d_stem_rows(at, row):
        d_stem = dot_f32(windows(dy1_pad, at), turned[...]) + get(dy2_pad, at).astype(jnp.float32)
        live = get(stem_pad, at).astype(jnp.float32) > 0
        dy = jnp.where(live, d_stem, 0.0).astype(jnp.bfloat16)
        hold(0, dy, None, at, row)
        stem_sum[...] += dot_f32(x_ref[pl.ds(row, rows), :].T, dy)

    over_rows(stem_rows)
    over_rows(inner_rows)
    over_rows(out_rows)
    g_head[...] = head_sum[...].astype(g_head.dtype)
    weight_gradient(inner_pad, 1)
    turn(1)
    over_rows(d_inner_rows)
    weight_gradient(stem_pad, 0)
    turn(0)
    over_rows(d_stem_rows)
    g_stem[...] = stem_sum[...].astype(g_stem.dtype)


def gradients_of(params, maps, heat, alive, count, height, width):
    stem_weight, conv_weight, head_weight, biases = params
    positions, requests, features = maps.shape
    pixels, channels = head_weight.shape
    lanes = -(-pixels // LANES) * LANES
    total = positions * requests
    scale = alive * (2.0 / (count * (positions * pixels)))
    scale = jnp.pad(jnp.broadcast_to(scale[:, None], (requests, pixels)), ((0, 0), (0, lanes - pixels)))
    heat = jnp.pad(heat.reshape(total, pixels), ((0, 0), (0, lanes - pixels)))
    head = jnp.pad(head_weight, ((0, lanes - pixels), (0, 0)))
    padded = pltpu.VMEM((height + 2, width + 2, requests, channels), jnp.bfloat16)
    flops = 2 * total * channels * (6 * 9 * channels + 2 * features + 3 * lanes)
    g_stem, g_conv, g_head, g_bias = pl.pallas_call(
        functools.partial(step_kernel, height=height, width=width, step=2),
        out_shape=(
            jax.ShapeDtypeStruct(stem_weight.shape, jnp.bfloat16),
            jax.ShapeDtypeStruct(conv_weight.shape, jnp.bfloat16),
            jax.ShapeDtypeStruct(head.shape, jnp.bfloat16),
            jax.ShapeDtypeStruct(biases.shape, jnp.float32),
        ),
        in_specs=[pl.BlockSpec(memory_space=pltpu.VMEM)] * 7,
        out_specs=(pl.BlockSpec(memory_space=pltpu.VMEM),) * 4,
        scratch_shapes=[
            padded,
            padded,
            padded,
            padded,
            pltpu.VMEM((9 * channels, channels), jnp.bfloat16),
            pltpu.VMEM((channels, total), jnp.bfloat16),
            pltpu.VMEM(head.shape, jnp.float32),
            pltpu.VMEM(stem_weight.shape, jnp.float32),
        ],
        compiler_params=pltpu.CompilerParams(vmem_limit_bytes=48 * 2**20),
        cost_estimate=pl.CostEstimate(flops=flops, bytes_accessed=8 * 2**20, transcendentals=0),
    )(maps.reshape(total, features), heat, scale, stem_weight, conv_weight, head, biases)
    return g_stem, g_conv, g_head[:pixels], g_bias


MESH = pl.DeviceIdType.MESH


def exchange_kernel(
    asked_ref, shelf_ref, got_ref, table, parcel, landed, send_ask, recv_ask, send_map, recv_map, *, n_dev
):
    me = lax.axis_index("dev")
    samples = shelf_ref.shape[0]

    def ahead(offset):
        return lax.rem(me + offset, n_dev)

    def behind(offset):
        return lax.rem(me + n_dev - offset, n_dev)

    def each(body):
        def one(offset, carry):
            body(offset)
            return carry

        lax.fori_loop(1, n_dev, one, 0)

    barrier = pltpu.get_barrier_semaphore()
    each(
        lambda offset: pl.semaphore_signal(
            barrier, inc=1, device_id={"dev": ahead(offset)}, device_id_type=MESH
        )
    )
    pl.semaphore_wait(barrier, n_dev - 1)

    def ask(offset):
        return pltpu.make_async_remote_copy(
            src_ref=asked_ref.at[ahead(offset)],
            dst_ref=table.at[me],
            send_sem=send_ask.at[offset],
            recv_sem=recv_ask.at[offset],
            device_id={"dev": ahead(offset)},
            device_id_type=MESH,
        )

    def answer(offset):
        return pltpu.make_async_remote_copy(
            src_ref=parcel.at[behind(offset)],
            dst_ref=landed.at[me],
            send_sem=send_map.at[offset],
            recv_sem=recv_map.at[offset],
            device_id={"dev": behind(offset)},
            device_id_type=MESH,
        )

    def pack(wanted, box):
        picked = []
        for slot in range(CAP):
            total = jnp.zeros(shelf_ref.shape[1:], jnp.float32)
            for sample in range(samples):
                hit = wanted[slot : slot + 1, :] == sample
                total = jnp.where(hit, shelf_ref[sample], total)
            picked.append(total)
        box[...] = jnp.concatenate(picked, axis=0).astype(box.dtype)

    each(lambda offset: ask(offset).start())
    pack(asked_ref[me], landed.at[me])

    def reply(offset):
        ask(offset).wait_recv()
        pack(table[behind(offset)], parcel.at[behind(offset)])
        answer(offset).start()

    each(reply)

    def finish(offset):
        ask(offset).wait_send()
        answer(offset).wait_send()
        answer(offset).wait_recv()

    each(finish)
    got_ref[...] = landed[...]


def exchange(asked, power_maps, heat_maps, n_dev):
    samples, positions, features = power_maps.shape
    shelf = jnp.concatenate(
        [power_maps.reshape(samples, -1, LANES), heat_maps.reshape(samples, -1, LANES)], axis=1
    ).astype(jnp.float32)
    rows = shelf.shape[1]
    asked = jnp.pad(asked, ((0, 0), (0, 8 - CAP)), constant_values=-1)
    asked = jnp.broadcast_to(asked[:, :, None], (n_dev, 8, LANES))
    parcels = (n_dev, CAP * rows, LANES)
    got = pl.pallas_call(
        functools.partial(exchange_kernel, n_dev=n_dev),
        out_shape=jax.ShapeDtypeStruct(parcels, power_maps.dtype),
        in_specs=[pl.BlockSpec(memory_space=pltpu.VMEM)] * 2,
        out_specs=pl.BlockSpec(memory_space=pltpu.VMEM),
        scratch_shapes=[
            pltpu.VMEM((n_dev, 8, LANES), jnp.int32),
            pltpu.VMEM(parcels, power_maps.dtype),
            pltpu.VMEM(parcels, power_maps.dtype),
        ]
        + [pltpu.SemaphoreType.DMA((n_dev,))] * 4,
        compiler_params=pltpu.CompilerParams(
            collective_id=0, has_side_effects=True, vmem_limit_bytes=32 * 2**20
        ),
    )(asked, shelf)
    return got.reshape(n_dev * CAP, rows * LANES)


def route_requests(request_row, sample_count, home_row, store_size, slot_cap):
    lookup = request_row[:, None] == jnp.arange(home_row.shape[0], dtype=jnp.int32)[None, :]
    position = jnp.sum(jnp.where(lookup, home_row[None, :], 0), axis=1)
    owner_of = position // store_size
    local_of = position % store_size
    order_ids = jnp.arange(request_row.shape[0], dtype=jnp.int32)
    alive = order_ids < sample_count
    earlier = (
        (owner_of[:, None] == owner_of[None, :])
        & alive[None, :]
        & (order_ids[None, :] < order_ids[:, None])
    )
    slot_of = jnp.minimum(jnp.sum(earlier.astype(jnp.int32), axis=1), slot_cap - 1)
    return (owner_of, local_of, alive, slot_of)


def local(
    step_number,
    power_maps,
    heat_maps,
    home_table,
    requests,
    counts,
    stem_weight,
    conv_weight,
    head_weight,
    biases,
):
    n_dev = lax.axis_size("dev")
    store_size = power_maps.shape[0]
    home_row = home_table[0]
    owner_of, local_of, alive, slot_of = route_requests(
        requests[0], counts[0], home_row, store_size, CAP
    )
    slot_ids = jnp.arange(CAP, dtype=jnp.int32)
    owner_ids = jnp.arange(n_dev, dtype=jnp.int32)
    wanted = (
        (owner_of[:, None, None] == owner_ids[None, :, None])
        & alive[:, None, None]
        & (slot_of[:, None, None] == slot_ids[None, None, :])
    )
    asked = jnp.sum(jnp.where(wanted, local_of[:, None, None] + 1, 0), axis=0) - 1
    shard_params = (stem_weight, conv_weight, head_weight, biases)
    sent_params = as_sent(shard_params)
    bit_total = (n_dev * lax.axis_size("grp")).bit_length() - 1
    selector = step_number % bit_total

    got = exchange(asked, power_maps, heat_maps, n_dev)
    slots = jnp.arange(got.shape[0], dtype=jnp.int32)
    pick = (((owner_of * CAP + slot_of)[:, None] == slots[None, :]) & alive[:, None]).astype(got.dtype)
    batch = jnp.dot(pick, got, preferred_element_type=jnp.float32).astype(got.dtype)
    positions, features = power_maps.shape[1:]
    split = positions * features
    maps = batch[:, :split].reshape(-1, positions, features).swapaxes(0, 1)
    heat = batch[:, split:].reshape(batch.shape[0], positions, -1).swapaxes(0, 1)

    def branch(bit_number, sent, maps, heat):
        partner = partner_2(sent, ("grp", "dev"), bit_number)
        gradients = gradients_of(
            (sent[0][0], sent[1][0], sent[2][0], biases[0]),
            maps,
            heat,
            alive.astype(jnp.float32),
            counts[0].astype(jnp.float32),
            PH,
            PW,
        )
        updated = tuple(
            0.5 * (mine + theirs.astype(jnp.float32)) - LEARN_RATE * gradient[None].astype(jnp.float32)
            for mine, theirs, gradient in zip(shard_params, partner, gradients)
        )
        return updated + tuple(gradient[None].astype(jnp.bfloat16) for gradient in gradients)

    return lax.switch(
        selector, [functools.partial(branch, bit) for bit in range(bit_total)], sent_params, maps, heat
    )


def solution(mesh):
    placed = (
        P(),
        P(("grp", "dev"), None, None),
        P(("grp", "dev"), None),
        P("grp", None),
        P(("grp", "dev"), None),
        P(("grp", "dev")),
        P(("grp", "dev"), None, None),
        P(("grp", "dev"), None, None, None),
        P(("grp", "dev"), None, None),
        P(("grp", "dev"), None, None),
    )
    return jax.shard_map(
        local,
        mesh=mesh,
        in_specs=placed,
        out_specs=(
            P(("grp", "dev"), None, None),
            P(("grp", "dev"), None, None, None),
            P(("grp", "dev"), None, None),
            P(("grp", "dev"), None, None),
            P(("grp", "dev"), None, None),
            P(("grp", "dev"), None, None, None),
            P(("grp", "dev"), None, None),
            P(("grp", "dev"), None, None),
        ),
        check_vma=False,
    )
```

```python
import functools

import jax
import jax.numpy as jnp
from jax import lax
from jax.experimental import pallas as pl
from jax.experimental.pallas import tpu as pltpu
from jax.sharding import PartitionSpec as P

PH = 8
PW = 8
CAP = 2
LANES = 128


LEARN_RATE = 0.1


def as_sent(array):
    return jax.tree.map(lambda a: a.astype(jnp.bfloat16) if a.dtype == jnp.float32 else a, array)


def partner_2(array, axis, distance):
    return lax.ppermute(array, axis, [(i, i ^ 1 << distance) for i in range(lax.axis_size(axis))])


def dot_f32(a, b):
    return jnp.dot(a, b, preferred_element_type=jnp.float32)


def step_kernel(
    x_ref,
    heat_ref,
    scale_ref,
    stem_ref,
    conv_ref,
    head_ref,
    bias_ref,
    g_stem,
    g_conv,
    g_head,
    g_bias,
    stem_pad,
    inner_pad,
    dy2_pad,
    dy1_pad,
    turned,
    dy_turned,
    head_sum,
    stem_sum,
    *,
    height,
    width,
    step,
):
    requests, channels = stem_pad.shape[2:]
    rows = step * width * requests
    for pad in (stem_pad, inner_pad, dy2_pad, dy1_pad):
        edge_row = jnp.zeros((1,) + pad.shape[1:], pad.dtype)
        edge_col = jnp.zeros((pad.shape[0], 1) + pad.shape[2:], pad.dtype)
        pad[0:1] = edge_row
        pad[height + 1 : height + 2] = edge_row
        pad[:, 0:1] = edge_col
        pad[:, width + 1 : width + 2] = edge_col
    g_bias[...] = jnp.zeros_like(g_bias)
    head_sum[...] = jnp.zeros_like(head_sum)
    stem_sum[...] = jnp.zeros_like(stem_sum)

    def inside(pad, at):
        return pad.at[pl.ds(at + 1, step), 1 : width + 1]

    def put(pad, at, value):
        inside(pad, at)[...] = value.reshape(step, width, requests, channels)

    def get(pad, at):
        return inside(pad, at)[...].reshape(rows, channels)

    def windows(pad, at):
        return jnp.concatenate(
            [
                pad[pl.ds(at + i, step), j : j + width].reshape(rows, channels)
                for i in range(3)
                for j in range(3)
            ],
            axis=1,
        )

    def turn(which):
        for tap in range(9):
            turned[tap * channels : (tap + 1) * channels, :] = conv_ref[
                which, (8 - tap) * channels : (9 - tap) * channels, :
            ].T

    def over_rows(body):
        def one(chunk, carry):
            body(chunk * step, pl.multiple_of(chunk * rows, rows))
            return carry

        lax.fori_loop(0, height // step, one, 0)

    def weight_gradient(pad, which):
        def one(i, carry):
            for j in range(3):
                window = pad[pl.ds(i, height), j : j + width].reshape(-1, channels)
                product = dot_f32(dy_turned[...], window)
                start = pl.multiple_of((i * 3 + j) * channels, channels)
                g_conv[which, pl.ds(start, channels), :] = product.T.astype(g_conv.dtype)
            return carry

        lax.fori_loop(0, 3, one, 0)

    def hold(which, dy, pad, at, row):
        g_bias[which : which + 1, :] += jnp.sum(dy.astype(jnp.float32), axis=0, keepdims=True)
        if pad is not None:
            put(pad, at, dy)
            dy_turned[:, pl.ds(row, rows)] = dy.T

    def stem_rows(at, row):
        x = x_ref[pl.ds(row, rows), :]
        put(stem_pad, at, jax.nn.relu(dot_f32(x, stem_ref[...]) + bias_ref[0:1, :]).astype(x.dtype))

    def inner_rows(at, row):
        pre = dot_f32(windows(stem_pad, at), conv_ref[0]) + bias_ref[1:2, :]
        put(inner_pad, at, jax.nn.relu(pre).astype(inner_pad.dtype))

    def out_rows(at, row):
        branch = dot_f32(windows(inner_pad, at), conv_ref[1]) + bias_ref[2:3, :]
        block = jax.nn.relu(get(stem_pad, at).astype(jnp.float32) + branch).astype(jnp.bfloat16)
        predicted = lax.dot_general(
            block, head_ref[...], (((1,), (1,)), ((), ())), preferred_element_type=jnp.float32
        )
        error = predicted - heat_ref[pl.ds(row, rows), :].astype(jnp.float32)
        d_predicted = (error.reshape(step * width, requests, -1) * scale_ref[...][None]).reshape(
            rows, -1
        )
        d_predicted = d_predicted.astype(jnp.bfloat16)
        head_sum[...] += dot_f32(d_predicted.T, block)
        d_block = dot_f32(d_predicted, head_ref[...])
        dy = jnp.where(block.astype(jnp.float32) > 0, d_block, 0.0).astype(jnp.bfloat16)
        hold(2, dy, dy2_pad, at, row)

    def d_inner_rows(at, row):
        d_inner = dot_f32(windows(dy2_pad, at), turned[...])
        live = get(inner_pad, at).astype(jnp.float32) > 0
        hold(1, jnp.where(live, d_inner, 0.0).astype(jnp.bfloat16), dy1_pad, at, row)

    def d_stem_rows(at, row):
        d_stem = dot_f32(windows(dy1_pad, at), turned[...]) + get(dy2_pad, at).astype(jnp.float32)
        live = get(stem_pad, at).astype(jnp.float32) > 0
        dy = jnp.where(live, d_stem, 0.0).astype(jnp.bfloat16)
        hold(0, dy, None, at, row)
        stem_sum[...] += dot_f32(x_ref[pl.ds(row, rows), :].T, dy)

    over_rows(stem_rows)
    over_rows(inner_rows)
    over_rows(out_rows)
    g_head[...] = head_sum[...].astype(g_head.dtype)
    weight_gradient(inner_pad, 1)
    turn(1)
    over_rows(d_inner_rows)
    weight_gradient(stem_pad, 0)
    turn(0)
    over_rows(d_stem_rows)
    g_stem[...] = stem_sum[...].astype(g_stem.dtype)


def gradients_of(params, maps, heat, alive, count, height, width):
    stem_weight, conv_weight, head_weight, biases = params
    positions, requests, features = maps.shape
    pixels, channels = head_weight.shape
    lanes = -(-pixels // LANES) * LANES
    total = positions * requests
    scale = alive * (2.0 / (count * (positions * pixels)))
    scale = jnp.pad(jnp.broadcast_to(scale[:, None], (requests, pixels)), ((0, 0), (0, lanes - pixels)))
    heat = jnp.pad(heat.reshape(total, pixels), ((0, 0), (0, lanes - pixels)))
    head = jnp.pad(head_weight, ((0, lanes - pixels), (0, 0)))
    padded = pltpu.VMEM((height + 2, width + 2, requests, channels), jnp.bfloat16)
    flops = 2 * total * channels * (6 * 9 * channels + 2 * features + 3 * lanes)
    g_stem, g_conv, g_head, g_bias = pl.pallas_call(
        functools.partial(step_kernel, height=height, width=width, step=2),
        out_shape=(
            jax.ShapeDtypeStruct(stem_weight.shape, jnp.bfloat16),
            jax.ShapeDtypeStruct(conv_weight.shape, jnp.bfloat16),
            jax.ShapeDtypeStruct(head.shape, jnp.bfloat16),
            jax.ShapeDtypeStruct(biases.shape, jnp.float32),
        ),
        in_specs=[pl.BlockSpec(memory_space=pltpu.VMEM)] * 7,
        out_specs=(pl.BlockSpec(memory_space=pltpu.VMEM),) * 4,
        scratch_shapes=[
            padded,
            padded,
            padded,
            padded,
            pltpu.VMEM((9 * channels, channels), jnp.bfloat16),
            pltpu.VMEM((channels, total), jnp.bfloat16),
            pltpu.VMEM(head.shape, jnp.float32),
            pltpu.VMEM(stem_weight.shape, jnp.float32),
        ],
        compiler_params=pltpu.CompilerParams(vmem_limit_bytes=48 * 2**20),
        cost_estimate=pl.CostEstimate(flops=flops, bytes_accessed=8 * 2**20, transcendentals=0),
    )(maps.reshape(total, features), heat, scale, stem_weight, conv_weight, head, biases)
    return g_stem, g_conv, g_head[:pixels], g_bias


MESH = pl.DeviceIdType.MESH


def exchange_kernel(
    asked_ref, shelf_ref, got_ref, table, parcel, landed, send_ask, recv_ask, send_map, recv_map, *, n_dev
):
    me = lax.axis_index("dev")
    samples = shelf_ref.shape[0]

    def ahead(offset):
        return lax.rem(me + offset, n_dev)

    def behind(offset):
        return lax.rem(me + n_dev - offset, n_dev)

    def each(body):
        def one(offset, carry):
            body(offset)
            return carry

        lax.fori_loop(1, n_dev, one, 0)

    barrier = pltpu.get_barrier_semaphore()
    each(
        lambda offset: pl.semaphore_signal(
            barrier, inc=1, device_id={"dev": ahead(offset)}, device_id_type=MESH
        )
    )
    pl.semaphore_wait(barrier, n_dev - 1)

    def ask(offset):
        return pltpu.make_async_remote_copy(
            src_ref=asked_ref.at[ahead(offset)],
            dst_ref=table.at[me],
            send_sem=send_ask.at[offset],
            recv_sem=recv_ask.at[offset],
            device_id={"dev": ahead(offset)},
            device_id_type=MESH,
        )

    def answer(offset):
        return pltpu.make_async_remote_copy(
            src_ref=parcel.at[behind(offset)],
            dst_ref=landed.at[me],
            send_sem=send_map.at[offset],
            recv_sem=recv_map.at[offset],
            device_id={"dev": behind(offset)},
            device_id_type=MESH,
        )

    def pack(wanted, box):
        picked = []
        for slot in range(CAP):
            total = jnp.zeros(shelf_ref.shape[1:], jnp.float32)
            for sample in range(samples):
                hit = wanted[slot : slot + 1, :] == sample
                total = jnp.where(hit, shelf_ref[sample], total)
            picked.append(total)
        box[...] = jnp.concatenate(picked, axis=0).astype(box.dtype)

    each(lambda offset: ask(offset).start())
    pack(asked_ref[me], landed.at[me])

    def reply(offset):
        ask(offset).wait_recv()
        pack(table[behind(offset)], parcel.at[behind(offset)])
        answer(offset).start()

    each(reply)

    def finish(offset):
        ask(offset).wait_send()
        answer(offset).wait_send()
        answer(offset).wait_recv()

    each(finish)
    got_ref[...] = landed[...]


def exchange(asked, power_maps, heat_maps, n_dev, call_id):
    samples, positions, features = power_maps.shape
    shelf = jnp.concatenate(
        [power_maps.reshape(samples, -1, LANES), heat_maps.reshape(samples, -1, LANES)], axis=1
    ).astype(jnp.float32)
    rows = shelf.shape[1]
    asked = jnp.pad(asked, ((0, 0), (0, 8 - CAP)), constant_values=-1)
    asked = jnp.broadcast_to(asked[:, :, None], (n_dev, 8, LANES))
    parcels = (n_dev, CAP * rows, LANES)
    got = pl.pallas_call(
        functools.partial(exchange_kernel, n_dev=n_dev),
        out_shape=jax.ShapeDtypeStruct(parcels, power_maps.dtype),
        in_specs=[pl.BlockSpec(memory_space=pltpu.VMEM)] * 2,
        out_specs=pl.BlockSpec(memory_space=pltpu.VMEM),
        scratch_shapes=[
            pltpu.VMEM((n_dev, 8, LANES), jnp.int32),
            pltpu.VMEM(parcels, power_maps.dtype),
            pltpu.VMEM(parcels, power_maps.dtype),
        ]
        + [pltpu.SemaphoreType.DMA((n_dev,))] * 4,
        compiler_params=pltpu.CompilerParams(
            collective_id=call_id, has_side_effects=True, vmem_limit_bytes=32 * 2**20
        ),
    )(asked, shelf)
    return got.reshape(n_dev * CAP, rows * LANES)


def route_requests(request_row, sample_count, home_row, store_size, slot_cap):
    lookup = request_row[:, None] == jnp.arange(home_row.shape[0], dtype=jnp.int32)[None, :]
    position = jnp.sum(jnp.where(lookup, home_row[None, :], 0), axis=1)
    owner_of = position // store_size
    local_of = position % store_size
    order_ids = jnp.arange(request_row.shape[0], dtype=jnp.int32)
    alive = order_ids < sample_count
    earlier = (
        (owner_of[:, None] == owner_of[None, :])
        & alive[None, :]
        & (order_ids[None, :] < order_ids[:, None])
    )
    slot_of = jnp.minimum(jnp.sum(earlier.astype(jnp.int32), axis=1), slot_cap - 1)
    return (owner_of, local_of, alive, slot_of)


def local(
    step_number,
    power_maps,
    heat_maps,
    home_table,
    requests,
    counts,
    stem_weight,
    conv_weight,
    head_weight,
    biases,
):
    n_dev = lax.axis_size("dev")
    store_size = power_maps.shape[0]
    home_row = home_table[0]
    owner_of, local_of, alive, slot_of = route_requests(
        requests[0], counts[0], home_row, store_size, CAP
    )
    slot_ids = jnp.arange(CAP, dtype=jnp.int32)
    owner_ids = jnp.arange(n_dev, dtype=jnp.int32)
    wanted = (
        (owner_of[:, None, None] == owner_ids[None, :, None])
        & alive[:, None, None]
        & (slot_of[:, None, None] == slot_ids[None, None, :])
    )
    asked = jnp.sum(jnp.where(wanted, local_of[:, None, None] + 1, 0), axis=0) - 1
    shard_params = (stem_weight, conv_weight, head_weight, biases)
    sent_params = as_sent(shard_params)
    bit_total = (n_dev * lax.axis_size("grp")).bit_length() - 1
    selector = step_number % bit_total

    def branch(bit_number, sent):
        partner = partner_2(sent, ("grp", "dev"), bit_number)
        got = exchange(asked, power_maps, heat_maps, n_dev, bit_number)
        slots = jnp.arange(got.shape[0], dtype=jnp.int32)
        pick = (((owner_of * CAP + slot_of)[:, None] == slots[None, :]) & alive[:, None]).astype(got.dtype)
        batch = jnp.dot(pick, got, preferred_element_type=jnp.float32).astype(got.dtype)
        positions, features = power_maps.shape[1:]
        split = positions * features
        maps = batch[:, :split].reshape(-1, positions, features).swapaxes(0, 1)
        heat = batch[:, split:].reshape(batch.shape[0], positions, -1).swapaxes(0, 1)
        gradients = gradients_of(
            (sent[0][0], sent[1][0], sent[2][0], biases[0]),
            maps,
            heat,
            alive.astype(jnp.float32),
            counts[0].astype(jnp.float32),
            PH,
            PW,
        )
        updated = tuple(
            0.5 * (mine + theirs.astype(jnp.float32)) - LEARN_RATE * gradient[None].astype(jnp.float32)
            for mine, theirs, gradient in zip(shard_params, partner, gradients)
        )
        return updated + tuple(gradient[None].astype(jnp.bfloat16) for gradient in gradients)

    return lax.switch(
        selector, [functools.partial(branch, bit) for bit in range(bit_total)], sent_params
    )


def solution(mesh):
    placed = (
        P(),
        P(("grp", "dev"), None, None),
        P(("grp", "dev"), None),
        P("grp", None),
        P(("grp", "dev"), None),
        P(("grp", "dev")),
        P(("grp", "dev"), None, None),
        P(("grp", "dev"), None, None, None),
        P(("grp", "dev"), None, None),
        P(("grp", "dev"), None, None),
    )
    return jax.shard_map(
        local,
        mesh=mesh,
        in_specs=placed,
        out_specs=(
            P(("grp", "dev"), None, None),
            P(("grp", "dev"), None, None, None),
            P(("grp", "dev"), None, None),
            P(("grp", "dev"), None, None),
            P(("grp", "dev"), None, None),
            P(("grp", "dev"), None, None, None),
            P(("grp", "dev"), None, None),
            P(("grp", "dev"), None, None),
        ),
        check_vma=False,
    )
```
